32 devices in a mesh: prod: 4 (over y, core), draw: 8 (over z, x).
Axes of the slice: x: 2, y: 2, z: 4, core: 2. Of those that a mesh axis runs over, the one named last changes fastest.
Arguments:
- product_traits: float32 [32, 262144], P(None, 'prod'), may hold values from -4 to 4
- mean_utility: float32 [262144], P('prod'), may hold values from -3 to 3
- target: float32 [262144], P('prod'), may hold values from -3 to 3
- taste_scale: float32 [32], replicated, may hold values from 0.02 to 0.2
- taste_draws: float32 [32, 2048], P(None, 'draw'), may hold values from -4 to 4
- outside: float32 [4, 2048], P(None, 'draw'), may hold values from -3 to 3
- block_market: int32 [1024], P('prod'), may hold values from 0 to 3
Outputs:
- mean_level: float32 [262144], P(('prod', 'draw'))
- residual: float32 [262144], P(('prod', 'draw'))
The draws below stay inside these ranges and needn't reach their ends.
All inputs are finite; a program needn't handle non-finite values.
Results may differ from the reference program's by a relative error of at most 0.0003.
Values sent between devices are 32-bit elements; how exact they have to be, the bound alone decides.
No kernel may reach another device: no remote copies, remote signals or barrier semaphores. Data moves between devices by JAX's collectives and lax.ppermute only.
A program may use at most 192 MiB of HBM per device.

```python
import math
import jax
import jax.numpy as jnp
from jax import lax

K = 32
MARKETS = 4
BLOCK = 256
ITERS = 2
R_DEV = 256
PRODUCTS = 262144
DRAWS = 2048
NBLK = 1024


def with_ends(array, key, low, largest):
    index_at = [jax.random.randint(jax.random.fold_in(key, axis), (), 0, length) for axis, length in enumerate(array.shape)]
    main_axis = array.shape.index(max(array.shape))
    neighbour = index_at[:main_axis] + [(index_at[main_axis] + 1) % array.shape[main_axis]] + index_at[main_axis + 1:]
    return array.at[tuple(index_at)].set(low).at[tuple(neighbour)].set(largest)


def levels(rng, extent, pieces, low, high):
    level, own = 1.0, jax.random.fold_in(rng, 6)
    for position, shards_of in pieces:
        steps = jnp.exp(jax.random.uniform(jax.random.fold_in(own, position), (shards_of,), jnp.float32, low / len(pieces), high / len(pieces)))
        level = level * jnp.repeat(steps, extent[position] // shards_of).reshape([-1 if axis == position else 1 for axis in range(len(extent))])
    return level


def bell_draw(rng, extent, deviation, limit, split=(), kind=jnp.bfloat16):
    gain = levels(rng, extent, split, -0.22, 0.18) if split else 1.0
    entries = jax.random.normal(rng, extent, jnp.float32) * deviation * gain
    return jnp.minimum(jnp.maximum(entries, -limit), limit).astype(kind)


def setup_inputs(seed: int = 0) -> dict:
    arg_keys = jax.random.split(jax.random.key(seed), 8)
    product_traits = bell_draw(arg_keys[0], (K, PRODUCTS), 1.0, 4.0, ((1, 4),), jnp.float32)
    mean_utility = bell_draw(arg_keys[1], (PRODUCTS,), 1.0, 3.0, ((0, 4),), jnp.float32)
    target = bell_draw(arg_keys[2], (PRODUCTS,), 0.5, 3.0, ((0, 4),), jnp.float32)
    taste_scale = jnp.clip(jnp.exp(jax.random.uniform(arg_keys[3], (K,), jnp.float32, math.log(0.02), math.log(0.2))), 0.02, 0.2)
    taste_draws = bell_draw(arg_keys[4], (K, DRAWS), 1.0, 4.0, ((1, 8),), jnp.float32)
    outside = bell_draw(arg_keys[5], (MARKETS, DRAWS), 1.0, 3.0, ((1, 8),), jnp.float32)
    block_market = with_ends(jax.random.randint(arg_keys[6], (NBLK,), 0, MARKETS), jax.random.fold_in(arg_keys[6], 1), 0, MARKETS - 1).astype(jnp.int32)
    return {"product_traits": product_traits, "mean_utility": mean_utility, "target": target, "taste_scale": taste_scale, "taste_draws": taste_draws, "outside": outside, "block_market": block_market}


def reference(product_traits, mean_utility, target, taste_scale, taste_draws, outside, block_market):
    onehot = (block_market[:, None] == jnp.arange(MARKETS, dtype=jnp.int32)[None, :]).astype(jnp.float32)
    market_scale = float(PRODUCTS // MARKETS)
    taste_mix = taste_scale[:, None] * taste_draws
    mean_level = mean_utility
    residual = jnp.zeros_like(mean_utility)
    group_ids = jnp.arange(DRAWS // R_DEV, dtype=jnp.int32)
    for sweep_index in range(ITERS):
        level_now = mean_level

        def draw_group(running, group_index):
            start = (group_index * R_DEV).astype(jnp.int32)
            mix_group = lax.dynamic_slice_in_dim(taste_mix, start, R_DEV, 1)
            out_group = lax.dynamic_slice_in_dim(outside, start, R_DEV, 1)
            spread = jnp.dot(mix_group.T, product_traits, precision=lax.Precision.HIGHEST, preferred_element_type=jnp.float32)
            expo = jnp.exp(level_now[None, :] + spread)
            shaped = expo.reshape(R_DEV, NBLK, BLOCK)
            denominator = jnp.dot(shaped.sum(axis=2), onehot, precision=lax.Precision.HIGHEST) + (market_scale * jnp.exp(out_group)).T
            per_block = jnp.dot(1.0 / denominator, onehot.T, precision=lax.Precision.HIGHEST)
            terms = jnp.einsum("rnb,rn->nb", shaped, per_block, precision=lax.Precision.HIGHEST).reshape(-1)
            return running + terms, None

        shares, unused = lax.scan(draw_group, jnp.zeros(PRODUCTS, jnp.float32), group_ids)
        shares = shares / float(DRAWS)
        residual = target - jnp.log(market_scale * shares)
        mean_level = mean_level + residual
    return mean_level, residual
```

```python
import functools
import math

import jax
import jax.numpy as jnp
from jax import lax
from jax.experimental import pallas as pl
from jax.experimental.pallas import tpu as pltpu
from jax.sharding import PartitionSpec as P

MARKETS = 4
BLOCK = 256
LANES = 128
HALVES = BLOCK // LANES
LOG2E = math.log2(math.e)
BUDGET = 58 * 2**20
FLOOR = 8 * 2**20
PIECES = 3
STEP_BLOCKS = 32
F32 = jnp.float32
BF16 = jnp.bfloat16
VMEM = pl.BlockSpec(memory_space=pltpu.VMEM)
SMEM = pl.BlockSpec(memory_space=pltpu.SMEM)
ANY = pl.BlockSpec(memory_space=pl.ANY)


def params(*shapes):
    return pltpu.CompilerParams(vmem_limit_bytes=sum(4 * math.prod(shape) for shape in shapes) + 2**20)


def rounded(values):
    return values.astype(BF16).astype(F32)


def top_rows(rows, columns):
    index = lax.broadcasted_iota(jnp.int32, (16, columns), 0)
    tile = jnp.zeros((16, columns), F32)
    for place, row in enumerate(rows):
        tile = jnp.where(index == place, row, tile)
    return tile


def trait_rows(traits, level):
    first = rounded(traits)
    second = traits - first
    scaled = level * LOG2E
    one = rounded(scaled)
    two = rounded(scaled - one)
    three = scaled - one - two
    return [first, second, first, top_rows((one, two, three), traits.shape[1])]


def taste_rows(taste_draws, scale_row):
    k_count, columns = taste_draws.shape
    diagonal = lax.broadcasted_iota(jnp.int32, (k_count, k_count), 0) == lax.broadcasted_iota(
        jnp.int32, (k_count, k_count), 1
    )
    scale = jnp.sum(jnp.where(diagonal, scale_row, 0.0), axis=1, keepdims=True)
    mix = scale * taste_draws * LOG2E
    first = rounded(mix)
    second = mix - first
    one = jnp.ones((1, columns), F32)
    return [first, first, second, top_rows((one, one, one), columns)]


def stacked(rows):
    return jnp.concatenate([row.astype(BF16) for row in rows], axis=0)


def level_row(level_ref, block):
    return jnp.concatenate(
        [level_ref[pl.ds(block * HALVES + half, 1), :] for half in range(HALVES)], axis=1
    )


def mm(left, right):
    return lax.dot_general(left, right, (((1,), (0,)), ((), ())), preferred_element_type=F32)


def first_sums(market_scale, market_ref, traits_ref, level_ref, scale_ref, draws_ref, outside_ref, sums_ref, left, total):
    step = pl.program_id(0)

    @pl.when(step == 0)
    def _():
        rows = jnp.concatenate(taste_rows(draws_ref[...], scale_ref[...]), axis=0)
        left[...] = rows.T.astype(BF16)
        total[...] = jnp.zeros_like(total)

    for local in range(traits_ref.shape[1] // BLOCK):
        block = step * (traits_ref.shape[1] // BLOCK) + local
        right = stacked(
            trait_rows(traits_ref[:, local * BLOCK : (local + 1) * BLOCK], level_row(level_ref, local))
        )
        expo = jnp.exp2(mm(left[...], right))
        part = expo[:, :LANES]
        for half in range(1, HALVES):
            part = part + expo[:, half * LANES : (half + 1) * LANES]
        market = market_ref[block]
        total[market] += part

    @pl.when(step == pl.num_programs(0) - 1)
    def _():
        own = jnp.where(lax.axis_index("prod") == 0, market_scale, 0.0)
        outer = own * jnp.exp(outside_ref[...])
        ones = jnp.ones((8, LANES), F32)
        pieces = []
        for market in range(MARKETS):
            summed = lax.dot_general(
                ones,
                total[market],
                (((1,), (1,)), ((), ())),
                precision=lax.Precision.HIGHEST,
                preferred_element_type=F32,
            )
            row = summed[0:1, :] + outer[market : market + 1, :]
            for half in range(row.shape[1] // LANES):
                pieces.append(row[:, half * LANES : (half + 1) * LANES])
        sums_ref[...] = jnp.concatenate(pieces, axis=0)


def split_products(traits_hbm, level_ref, traits_out, traits_vmem, arrived):
    part_len = traits_vmem.shape[1]
    own = lax.axis_index("draw")
    copy = pltpu.make_async_copy(
        traits_hbm.at[:, pl.ds(pl.multiple_of(own * part_len, part_len), part_len)], traits_vmem, arrived
    )
    copy.start()
    copy.wait()
    blocks = part_len // BLOCK

    def step(block, carry):
        start = pl.multiple_of(block * BLOCK, BLOCK)
        rows = trait_rows(traits_vmem[:, pl.ds(start, BLOCK)], level_row(level_ref, own * blocks + block))
        traits_out[pl.ds(start, BLOCK), :] = jnp.concatenate(rows, axis=0).T.astype(BF16)
        return carry

    lax.fori_loop(0, blocks, step, 0, unroll=2)


def group_at(place, stages):
    own = lax.axis_index("draw")
    group = own
    for stride, factor in stages:
        digit = lax.rem(own // stride, factor)
        shift = place % factor
        place //= factor
        group = group + (lax.rem(digit - shift + factor, factor) - digit) * stride
    return group


def split_draws(count, scale_ref, *refs):
    draws_refs, right_out = refs[:count], refs[count]
    group = draws_refs[0].shape[2]
    index = 0
    for ref in draws_refs:
        for place in range(ref.shape[0]):
            right_out[:, index * group : (index + 1) * group] = stacked(taste_rows(ref[place], scale_ref[...]))
            index += 1


def fill(offset, traits_ref, right_ref, expo_ref):
    blocks, kept = expo_ref.shape[0] // BLOCK, expo_ref.shape[1]

    def step(block, carry):
        start = pl.multiple_of(block * BLOCK, BLOCK)
        left = traits_ref[pl.ds(start, BLOCK), :]

        def columns(begin):
            expo_ref[pl.ds(start, BLOCK), pl.ds(begin, 256)] = jnp.exp2(mm(left, right_ref[:, pl.ds(offset + begin, 256)]))

        if kept <= 2048:
            for begin in range(0, kept, 256):
                columns(begin)
        else:

            def inner(index, carry):
                columns(pl.multiple_of(index * 256, 256))
                return carry

            lax.fori_loop(0, kept // 256, inner, 0)
        return carry

    lax.fori_loop(0, blocks, step, 0, unroll=4)


def inverse_rows(inverse, pieces):
    for group, tile in enumerate(pieces):
        flipped = 1.0 / tile
        halves = tile.shape[0] // MARKETS
        for market in range(MARKETS):
            for half in range(halves):
                row = market * halves + half
                start = (group * halves + half) * LANES
                inverse[market, 0:1, start : start + LANES] = flipped[row : row + 1, :]


def over_columns(width, body, carry):
    tiles = width // LANES
    if tiles <= 16:
        for tile in range(tiles):
            carry = body(tile * LANES, carry)
        return carry
    return lax.fori_loop(0, tiles, lambda tile, kept: body(pl.multiple_of(tile * LANES, LANES), kept), carry)


def share_sum(expo_refs, rest_expo, inverse, market, start):
    total = jnp.zeros((BLOCK, LANES), F32)
    offset = 0
    for ref in expo_refs + (rest_expo,):
        first = 0 if ref is rest_expo else start

        def columns(begin, total, ref=ref, first=first, offset=offset):
            terms = ref[pl.ds(first, BLOCK), pl.ds(begin, LANES)]
            return total + terms * inverse[market, 0:1, pl.ds(offset + begin, LANES)]

        total = over_columns(ref.shape[1], columns, total)
        offset += ref.shape[1]
    return jnp.sum(total, axis=1, keepdims=True)


def rest_columns_of(rest_expo, traits_ref, rest_ref, start):
    left = traits_ref[pl.ds(start, BLOCK), :]
    for begin in range(0, rest_expo.shape[1], 256):
        rest_expo[:, begin : begin + 256] = jnp.exp2(mm(left, rest_ref[:, pl.ds(rest_ref.shape[1] - rest_expo.shape[1] + begin, 256)]))


def own_rows(ref, blocks):
    base = lax.axis_index("draw") * (blocks * HALVES)
    return jnp.concatenate(
        [ref[pl.ds(base + half, blocks, stride=HALVES), :] for half in range(HALVES)], axis=1
    )


def both_sums(market_scale, share_scale, stages, counts, market_ref, *refs):
    sums_refs, refs = refs[: counts[0]], refs[counts[0] :]
    (target_ref, outside_ref, traits_ref, right_ref), refs = refs[:4], refs[4:]
    expo_refs, refs = refs[: counts[1]], refs[counts[1] :]
    share_ref, next_ref, inverse, total, growth, rest_expo = refs
    blocks = expo_refs[0].shape[0] // BLOCK
    groups = next_ref.shape[0]
    own = lax.axis_index("draw")
    inverse_rows(inverse, [ref[place] for ref in sums_refs for place in range(ref.shape[0])])
    total[...] = jnp.zeros_like(total)
    wanted = jnp.exp(own_rows(target_ref, blocks)) / share_scale
    if blocks < LANES:
        wanted = jnp.concatenate([wanted, jnp.ones((LANES - blocks, BLOCK), F32)], axis=0)
    growth[...] = wanted.T
    share_ref[...] = jnp.ones_like(share_ref)
    lane = lax.broadcasted_iota(jnp.int32, (BLOCK, LANES), 1)

    def step(block, carry):
        start = pl.multiple_of(block * BLOCK, BLOCK)
        market = market_ref[own * blocks + block]
        rest_columns_of(rest_expo, traits_ref, right_ref, start)
        share = share_sum(expo_refs, rest_expo, inverse, market, start)
        here = lane == block
        factor = jnp.sum(jnp.where(here, growth[...], 0.0), axis=1, keepdims=True)
        share_ref[...] = jnp.where(here, share, share_ref[...])
        factor = jnp.broadcast_to(factor / share, (BLOCK, LANES))
        offset = 0
        for ref in expo_refs + (rest_expo,):
            first = 0 if ref is rest_expo else start

            def columns(begin, carry, ref=ref, first=first, offset=offset):
                terms = ref[pl.ds(first, BLOCK), pl.ds(begin, LANES)] * factor
                total[market, :, pl.ds(offset + begin, LANES)] += terms.reshape(BLOCK // 8, 8, LANES).sum(axis=0)
                return carry

            over_columns(ref.shape[1], columns, 0)
            offset += ref.shape[1]
        return carry

    lax.fori_loop(0, blocks, step, 0, unroll=2)
    halves = next_ref.shape[1] // MARKETS
    mine = jnp.where(lax.axis_index("prod") == 0, market_scale, 0.0)
    outer = mine * jnp.exp(outside_ref[...])
    for place in range(groups):
        rows = []
        for market in range(MARKETS):
            for half in range(halves):
                begin = (place * halves + half) * LANES
                row = jnp.sum(total[market, :, begin : begin + LANES], axis=0, keepdims=True)
                if place == 0:
                    row = row + outer[market : market + 1, half * LANES : (half + 1) * LANES]
                rows.append(row)
        next_ref[group_at(place, stages)] = jnp.concatenate(rows, axis=0)


def last_sums(share_scale, stages, counts, market_ref, *refs):
    sums_refs, refs = refs[: counts[0]], refs[counts[0] :]
    (target_ref, level_ref, traits_ref, right_ref), refs = refs[:4], refs[4:]
    expo_refs, refs = refs[: counts[1]], refs[counts[1] :]
    share_ref, out_level, out_residual, inverse, second, rest_expo = refs
    blocks = expo_refs[0].shape[0] // BLOCK
    own = lax.axis_index("draw")
    pieces = []
    for place in range(sums_refs[0].shape[0]):
        group = group_at(place, stages)
        tile = sums_refs[0][group]
        for ref in sums_refs[1:]:
            tile = tile + ref[group]
        pieces.append(tile)
    inverse_rows(inverse, pieces)
    second[...] = jnp.ones_like(second)
    lane = lax.broadcasted_iota(jnp.int32, (BLOCK, LANES), 1)

    def step(block, carry):
        start = pl.multiple_of(block * BLOCK, BLOCK)
        market = market_ref[own * blocks + block]
        rest_columns_of(rest_expo, traits_ref, right_ref, start)
        share = share_sum(expo_refs, rest_expo, inverse, market, start)
        second[...] = jnp.where(lane == block, share, second[...])
        return carry

    lax.fori_loop(0, blocks, step, 0, unroll=2)
    before = share_ref[...].T[:blocks]
    after = second[...].T[:blocks]
    residual = jnp.log(before) - jnp.log(after)
    level = own_rows(level_ref, blocks) + own_rows(target_ref, blocks) - jnp.log(after * share_scale)
    for half in range(HALVES):
        columns = slice(half * LANES, (half + 1) * LANES)
        out_residual[pl.ds(half, blocks, stride=HALVES), :] = residual[:, columns]
        out_level[pl.ds(half, blocks, stride=HALVES), :] = level[:, columns]


def digit_pairs(size, stride, factor, shift):
    pairs = []
    for index in range(size):
        digit = index // stride % factor
        pairs.append((index, index + ((digit + shift) % factor - digit) * stride))
    return pairs


def shifted(values, axis, stride, factor):
    size = lax.axis_size(axis)
    return [values] + [
        lax.ppermute(values, axis, digit_pairs(size, stride, factor, shift)) for shift in range(1, factor)
    ]


def collected(values, stages):
    parts = [values[None]]
    for stride, factor in stages:
        joined = parts[0] if len(parts) == 1 else jnp.concatenate(parts, axis=0)
        parts = shifted(joined, "draw", stride, factor)
    return parts


def total_of(parts):
    return functools.reduce(jnp.add, parts)


def body(product_traits, mean_utility, target, taste_scale, taste_draws, outside, block_market):
    k_count, prod_count = product_traits.shape
    group = taste_draws.shape[1]
    draw_devices = lax.axis_size("draw")
    prod_devices = lax.axis_size("prod")
    draws = group * draw_devices
    market_scale = float(prod_count * prod_devices // MARKETS)
    share_scale = market_scale / float(draws)
    part_len = prod_count // draw_devices
    depth = 3 * k_count + 16
    tile_rows = MARKETS * group // LANES
    cells = prod_count * group

    level_rows = mean_utility.reshape(-1, LANES)
    target_rows = target.reshape(-1, LANES)
    scale_row = taste_scale.reshape(1, k_count)

    stages = []
    stride = 1
    while stride < draw_devices:
        factor = 2 if stride == 1 else math.gcd(4, draw_devices // stride)
        stages.append((stride, factor))
        stride *= factor

    def grant(rest):
        return 4 * (draws * MARKETS * 16 + BLOCK * rest + 2**19)

    fixed = 2 * depth * draws + 2 * LANES * part_len
    eighths = max(
        count for count in range(1, 8) if fixed + draws // 8 * count * part_len * 4 + grant(draws - draws // 8 * count) < BUDGET
    )
    kept = draws // 8 * eighths
    rest = draws - kept
    bounds = [draws // 8 * (eighths * index // PIECES) for index in range(PIECES + 1)]
    held_params = pltpu.CompilerParams(vmem_limit_bytes=max(grant(rest), FLOOR))

    every_draw = collected(taste_draws, stages)

    step_len = min(STEP_BLOCKS * BLOCK, prod_count)
    whole = lambda shape: pl.BlockSpec(shape, lambda step, market: (0,) * len(shape))
    first = pl.pallas_call(
        functools.partial(first_sums, market_scale),
        grid_spec=pltpu.PrefetchScalarGridSpec(
            num_scalar_prefetch=1,
            grid=(prod_count // step_len,),
            in_specs=[
                pl.BlockSpec((k_count, step_len), lambda step, market: (0, step)),
                pl.BlockSpec((step_len // LANES, LANES), lambda step, market: (step, 0)),
                whole((1, k_count)),
                whole((k_count, group)),
                whole((MARKETS, group)),
            ],
            out_specs=whole((tile_rows, LANES)),
            scratch_shapes=[
                pltpu.VMEM((group, depth), BF16),
                pltpu.VMEM((MARKETS, group, LANES), F32),
            ],
        ),
        out_shape=jax.ShapeDtypeStruct((tile_rows, LANES), F32),
        compiler_params=params((k_count, step_len), (k_count, step_len), (MARKETS, group, LANES), (BLOCK, step_len), (2**20,)),
        cost_estimate=pl.CostEstimate(flops=2 * cells * 256, bytes_accessed=4 * k_count * prod_count, transcendentals=cells),
        name="first_sums",
    )(*[pltpu.with_memory_space_constraint(array, pltpu.HBM) for array in (block_market, product_traits, level_rows, scale_row, taste_draws, outside)])

    sums = collected(total_of(shifted(first, "prod", 1, prod_devices)), stages)

    hbm_traits = pltpu.with_memory_space_constraint(product_traits, pltpu.HBM)
    traits_split = pl.pallas_call(
        split_products,
        in_specs=[ANY, VMEM],
        out_specs=VMEM,
        out_shape=pltpu.VMEM((part_len, depth), BF16),
        scratch_shapes=[pltpu.VMEM((k_count, part_len), F32), pltpu.SemaphoreType.DMA],
        compiler_params=params((k_count, part_len), (prod_count,), (depth, part_len)),
        name="split_products",
    )(hbm_traits, level_rows)
    draws_split = pl.pallas_call(
        functools.partial(split_draws, len(every_draw)),
        in_specs=[VMEM] * (1 + len(every_draw)),
        out_specs=VMEM,
        out_shape=pltpu.VMEM((depth, draws), BF16),
        compiler_params=params((k_count, draws), (depth, draws)),
        name="split_draws",
    )(scale_row, *every_draw)
    traits_split, draws_split = [
        pltpu.with_memory_space_constraint(array, pltpu.VMEM) for array in (traits_split, draws_split)
    ]
    expo = []
    for begin, end in zip(bounds, bounds[1:]):
        piece = pl.pallas_call(
            functools.partial(fill, begin),
            in_specs=[VMEM, VMEM],
            out_specs=VMEM,
            out_shape=pltpu.VMEM((part_len, end - begin), F32),
            compiler_params=held_params,
            cost_estimate=pl.CostEstimate(
                flops=2 * part_len * (end - begin) * 256, bytes_accessed=2**20, transcendentals=part_len * (end - begin)
            ),
            name="fill",
        )(traits_split, draws_split)
        expo.append(pltpu.with_memory_space_constraint(piece, pltpu.VMEM))
    held = (traits_split, draws_split, *expo)

    share, partial = pl.pallas_call(
        functools.partial(both_sums, market_scale, share_scale, stages, (len(sums), len(expo))),
        in_specs=[SMEM] + [VMEM] * (len(sums) + 4 + len(expo)),
        out_specs=(VMEM, VMEM),
        out_shape=(
            jax.ShapeDtypeStruct((BLOCK, LANES), F32),
            jax.ShapeDtypeStruct((draw_devices, tile_rows, LANES), F32),
        ),
        scratch_shapes=[
            pltpu.VMEM((MARKETS, 8, draws), F32),
            pltpu.VMEM((MARKETS, 8, draws), F32),
            pltpu.VMEM((BLOCK, LANES), F32),
            pltpu.VMEM((BLOCK, rest), F32),
        ],
        compiler_params=held_params,
        cost_estimate=pl.CostEstimate(flops=4 * cells, bytes_accessed=2**20, transcendentals=0),
        name="both_sums",
    )(block_market, *sums, target_rows, outside, *held)

    parts = shifted(partial, "prod", 1, prod_devices)
    for stride, factor in stages:
        parts = shifted(total_of(parts), "draw", stride, factor)

    level, residual = pl.pallas_call(
        functools.partial(last_sums, share_scale, stages, (len(parts), len(expo))),
        in_specs=[SMEM] + [VMEM] * (len(parts) + 4 + len(expo) + 1),
        out_specs=(VMEM, VMEM),
        out_shape=(jax.ShapeDtypeStruct((part_len // LANES, LANES), F32),) * 2,
        scratch_shapes=[
            pltpu.VMEM((MARKETS, 8, draws), F32),
            pltpu.VMEM((BLOCK, LANES), F32),
            pltpu.VMEM((BLOCK, rest), F32),
        ],
        compiler_params=held_params,
        cost_estimate=pl.CostEstimate(flops=2 * cells, bytes_accessed=2**20, transcendentals=0),
        name="last_sums",
    )(block_market, *parts, target_rows, level_rows, *held, share)
    return level.reshape(-1), residual.reshape(-1)


def solution(mesh):
    placed = (
        P(None, "prod"),
        P("prod"),
        P("prod"),
        P(),
        P(None, "draw"),
        P(None, "draw"),
        P("prod"),
    )
    return jax.shard_map(
        body,
        mesh=mesh,
        in_specs=placed,
        out_specs=(P(("prod", "draw")), P(("prod", "draw"))),
        check_vma=False,
    )
```

```python
import functools
import math

import jax
import jax.numpy as jnp
from jax import lax
from jax.experimental import pallas as pl
from jax.experimental.pallas import tpu as pltpu
from jax.sharding import PartitionSpec as P

MARKETS = 4
BLOCK = 256
LANES = 128
HALVES = BLOCK // LANES
LOG2E = math.log2(math.e)
BUDGET = 58 * 2**20
FLOOR = 10 * 2**20
PIECES = 3
STEP_BLOCKS = 32
F32 = jnp.float32
BF16 = jnp.bfloat16
VMEM = pl.BlockSpec(memory_space=pltpu.VMEM)
SMEM = pl.BlockSpec(memory_space=pltpu.SMEM)
ANY = pl.BlockSpec(memory_space=pl.ANY)


def params(*shapes):
    return pltpu.CompilerParams(vmem_limit_bytes=sum(4 * math.prod(shape) for shape in shapes) + 2**20)


def rounded(values):
    return values.astype(BF16).astype(F32)


def top_rows(rows, columns):
    index = lax.broadcasted_iota(jnp.int32, (16, columns), 0)
    tile = jnp.zeros((16, columns), F32)
    for place, row in enumerate(rows):
        tile = jnp.where(index == place, row, tile)
    return tile


def trait_rows(traits, level):
    first = rounded(traits)
    second = traits - first
    scaled = level * LOG2E
    one = rounded(scaled)
    two = rounded(scaled - one)
    three = scaled - one - two
    return [first, second, first, top_rows((one, two, three), traits.shape[1])]


def taste_rows(taste_draws, scale_row):
    k_count, columns = taste_draws.shape
    diagonal = lax.broadcasted_iota(jnp.int32, (k_count, k_count), 0) == lax.broadcasted_iota(
        jnp.int32, (k_count, k_count), 1
    )
    scale = jnp.sum(jnp.where(diagonal, scale_row, 0.0), axis=1, keepdims=True)
    mix = scale * taste_draws * LOG2E
    first = rounded(mix)
    second = mix - first
    one = jnp.ones((1, columns), F32)
    return [first, first, second, top_rows((one, one, one), columns)]


def stacked(rows):
    return jnp.concatenate([row.astype(BF16) for row in rows], axis=0)


def level_row(level_ref, block):
    return jnp.concatenate(
        [level_ref[pl.ds(block * HALVES + half, 1), :] for half in range(HALVES)], axis=1
    )


def mm(left, right):
    return lax.dot_general(left, right, (((1,), (0,)), ((), ())), preferred_element_type=F32)


def first_sums(market_scale, begin, market_ref, traits_ref, level_ref, scale_ref, draws_ref, before_ref, sums_ref, left, total):
    step = pl.program_id(0)

    @pl.when(step == 0)
    def _():
        rows = jnp.concatenate(taste_rows(draws_ref[...], scale_ref[...]), axis=0)
        left[...] = rows.T.astype(BF16)
        total[...] = jnp.zeros_like(total)

    for local in range(traits_ref.shape[1] // BLOCK):
        block = (begin + step) * (traits_ref.shape[1] // BLOCK) + local
        right = stacked(
            trait_rows(traits_ref[:, local * BLOCK : (local + 1) * BLOCK], level_row(level_ref, local))
        )
        expo = jnp.exp2(mm(left[...], right))
        part = expo[:, :LANES]
        for half in range(1, HALVES):
            part = part + expo[:, half * LANES : (half + 1) * LANES]
        market = market_ref[block]
        total[market] += part

    @pl.when(step == pl.num_programs(0) - 1)
    def _():
        if begin == 0:
            own = jnp.where(lax.axis_index("prod") == 0, market_scale, 0.0)
            outer = own * jnp.exp(before_ref[...])
        ones = jnp.ones((8, LANES), F32)
        pieces = []
        for market in range(MARKETS):
            summed = lax.dot_general(
                ones,
                total[market],
                (((1,), (1,)), ((), ())),
                precision=lax.Precision.HIGHEST,
                preferred_element_type=F32,
            )
            row = summed[0:1, :]
            if begin == 0:
                row = row + outer[market : market + 1, :]
            for half in range(row.shape[1] // LANES):
                pieces.append(row[:, half * LANES : (half + 1) * LANES])
        tile = jnp.concatenate(pieces, axis=0)
        sums_ref[...] = tile if begin == 0 else tile + before_ref[...]


def split_products(traits_hbm, level_ref, traits_out, traits_vmem, arrived):
    part_len = traits_vmem.shape[1]
    own = lax.axis_index("draw")
    copy = pltpu.make_async_copy(
        traits_hbm.at[:, pl.ds(pl.multiple_of(own * part_len, part_len), part_len)], traits_vmem, arrived
    )
    copy.start()
    copy.wait()
    blocks = part_len // BLOCK

    def step(block, carry):
        start = pl.multiple_of(block * BLOCK, BLOCK)
        rows = trait_rows(traits_vmem[:, pl.ds(start, BLOCK)], level_row(level_ref, own * blocks + block))
        traits_out[pl.ds(start, BLOCK), :] = jnp.concatenate(rows, axis=0).T.astype(BF16)
        return carry

    lax.fori_loop(0, blocks, step, 0, unroll=2)


def group_at(place, stages):
    own = lax.axis_index("draw")
    group = own
    for stride, factor in stages:
        digit = lax.rem(own // stride, factor)
        shift = place % factor
        place //= factor
        group = group + (lax.rem(digit - shift + factor, factor) - digit) * stride
    return group


def split_draws(stages, scale_ref, draws_ref, right_out):
    group = draws_ref.shape[2]
    for place in range(draws_ref.shape[0]):
        rows = taste_rows(draws_ref[group_at(place, stages)], scale_ref[...])
        right_out[:, place * group : (place + 1) * group] = stacked(rows)


def fill(offset, traits_ref, right_ref, expo_ref):
    blocks, kept = expo_ref.shape[0] // BLOCK, expo_ref.shape[1]

    def step(block, carry):
        start = pl.multiple_of(block * BLOCK, BLOCK)
        left = traits_ref[pl.ds(start, BLOCK), :]

        def columns(begin):
            expo_ref[pl.ds(start, BLOCK), pl.ds(begin, 256)] = jnp.exp2(mm(left, right_ref[:, pl.ds(offset + begin, 256)]))

        if kept <= 2048:
            for begin in range(0, kept, 256):
                columns(begin)
        else:

            def inner(index, carry):
                columns(pl.multiple_of(index * 256, 256))
                return carry

            lax.fori_loop(0, kept // 256, inner, 0)
        return carry

    lax.fori_loop(0, blocks, step, 0, unroll=4)


def inverse_rows(inverse, pieces):
    for group, tile in enumerate(pieces):
        flipped = 1.0 / tile
        halves = tile.shape[0] // MARKETS
        for market in range(MARKETS):
            for half in range(halves):
                row = market * halves + half
                start = (group * halves + half) * LANES
                inverse[market, :, start : start + LANES] = jnp.broadcast_to(flipped[row : row + 1, :], (8, LANES))


def over_columns(width, body, carry):
    tiles = width // LANES
    if tiles <= 16:
        for tile in range(tiles):
            carry = body(tile * LANES, carry)
        return carry
    return lax.fori_loop(0, tiles, lambda tile, kept: body(pl.multiple_of(tile * LANES, LANES), kept), carry)


def share_sum(expo_refs, rest_expo, inverse, market, start):
    total = jnp.zeros((BLOCK // 8, 8, LANES), F32)
    offset = 0
    for ref in expo_refs + (rest_expo,):
        first = 0 if ref is rest_expo else start

        def columns(begin, total, ref=ref, first=first, offset=offset):
            terms = ref[pl.ds(first, BLOCK), pl.ds(begin, LANES)].reshape(BLOCK // 8, 8, LANES)
            return total + terms * inverse[market, :, pl.ds(offset + begin, LANES)]

        total = over_columns(ref.shape[1], columns, total)
        offset += ref.shape[1]
    return jnp.sum(total.reshape(BLOCK, LANES), axis=1, keepdims=True)


def rest_columns_of(rest_expo, traits_ref, rest_ref, start):
    left = traits_ref[pl.ds(start, BLOCK), :]
    for begin in range(0, rest_expo.shape[1], 256):
        rest_expo[:, begin : begin + 256] = jnp.exp2(mm(left, rest_ref[:, pl.ds(rest_ref.shape[1] - rest_expo.shape[1] + begin, 256)]))


def own_rows(ref, blocks):
    base = lax.axis_index("draw") * (blocks * HALVES)
    return jnp.concatenate(
        [ref[pl.ds(base + half, blocks, stride=HALVES), :] for half in range(HALVES)], axis=1
    )


def both_sums(market_scale, share_scale, stages, counts, market_ref, *refs):
    sums_refs, refs = refs[: counts[0]], refs[counts[0] :]
    (target_ref, outside_ref, traits_ref, right_ref), refs = refs[:4], refs[4:]
    expo_refs, refs = refs[: counts[1]], refs[counts[1] :]
    share_ref, next_ref, inverse, total, growth, rest_expo = refs
    blocks = expo_refs[0].shape[0] // BLOCK
    groups = next_ref.shape[0]
    own = lax.axis_index("draw")
    inverse_rows(inverse, [ref[place] for ref in sums_refs for place in range(ref.shape[0])])
    total[...] = jnp.zeros_like(total)
    wanted = jnp.exp(own_rows(target_ref, blocks)) / share_scale
    if blocks < LANES:
        wanted = jnp.concatenate([wanted, jnp.ones((LANES - blocks, BLOCK), F32)], axis=0)
    growth[...] = wanted.T
    share_ref[...] = jnp.ones_like(share_ref)
    lane = lax.broadcasted_iota(jnp.int32, (BLOCK, LANES), 1)

    def step(block, carry):
        start = pl.multiple_of(block * BLOCK, BLOCK)
        market = market_ref[own * blocks + block]
        rest_columns_of(rest_expo, traits_ref, right_ref, start)
        share = share_sum(expo_refs, rest_expo, inverse, market, start)
        here = lane == block
        factor = jnp.sum(jnp.where(here, growth[...], 0.0), axis=1, keepdims=True)
        share_ref[...] = jnp.where(here, share, share_ref[...])
        factor = jnp.broadcast_to(factor / share, (BLOCK, LANES))
        offset = 0
        for ref in expo_refs + (rest_expo,):
            first = 0 if ref is rest_expo else start

            def columns(begin, carry, ref=ref, first=first, offset=offset):
                terms = ref[pl.ds(first, BLOCK), pl.ds(begin, LANES)] * factor
                total[market, :, pl.ds(offset + begin, LANES)] += terms.reshape(BLOCK // 8, 8, LANES).sum(axis=0)
                return carry

            over_columns(ref.shape[1], columns, 0)
            offset += ref.shape[1]
        return carry

    lax.fori_loop(0, blocks, step, 0, unroll=4)
    halves = next_ref.shape[1] // MARKETS
    mine = jnp.where(lax.axis_index("prod") == 0, market_scale, 0.0)
    outer = mine * jnp.exp(outside_ref[...])
    for place in range(groups):
        rows = []
        for market in range(MARKETS):
            for half in range(halves):
                begin = (place * halves + half) * LANES
                row = jnp.sum(total[market, :, begin : begin + LANES], axis=0, keepdims=True)
                if place == 0:
                    row = row + outer[market : market + 1, half * LANES : (half + 1) * LANES]
                rows.append(row)
        next_ref[group_at(place, stages)] = jnp.concatenate(rows, axis=0)


def last_sums(share_scale, stages, counts, market_ref, *refs):
    sums_refs, refs = refs[: counts[0]], refs[counts[0] :]
    (target_ref, level_ref, traits_ref, right_ref), refs = refs[:4], refs[4:]
    expo_refs, refs = refs[: counts[1]], refs[counts[1] :]
    share_ref, out_level, out_residual, inverse, second, rest_expo = refs
    blocks = expo_refs[0].shape[0] // BLOCK
    own = lax.axis_index("draw")
    pieces = []
    for place in range(sums_refs[0].shape[0]):
        group = group_at(place, stages)
        tile = sums_refs[0][group]
        for ref in sums_refs[1:]:
            tile = tile + ref[group]
        pieces.append(tile)
    inverse_rows(inverse, pieces)
    second[...] = jnp.ones_like(second)
    lane = lax.broadcasted_iota(jnp.int32, (BLOCK, LANES), 1)

    def step(block, carry):
        start = pl.multiple_of(block * BLOCK, BLOCK)
        market = market_ref[own * blocks + block]
        rest_columns_of(rest_expo, traits_ref, right_ref, start)
        share = share_sum(expo_refs, rest_expo, inverse, market, start)
        second[...] = jnp.where(lane == block, share, second[...])
        return carry

    lax.fori_loop(0, blocks, step, 0, unroll=4)
    before = share_ref[...].T[:blocks]
    after = second[...].T[:blocks]
    residual = jnp.log(before) - jnp.log(after)
    level = own_rows(level_ref, blocks) + own_rows(target_ref, blocks) - jnp.log(after * share_scale)
    for half in range(HALVES):
        columns = slice(half * LANES, (half + 1) * LANES)
        out_residual[pl.ds(half, blocks, stride=HALVES), :] = residual[:, columns]
        out_level[pl.ds(half, blocks, stride=HALVES), :] = level[:, columns]


def digit_pairs(size, stride, factor, shift):
    pairs = []
    for index in range(size):
        digit = index // stride % factor
        pairs.append((index, index + ((digit + shift) % factor - digit) * stride))
    return pairs


def shifted(values, axis, stride, factor):
    size = lax.axis_size(axis)
    return [values] + [
        lax.ppermute(values, axis, digit_pairs(size, stride, factor, shift)) for shift in range(1, factor)
    ]


def collected(parts, stages):
    for stride, factor in stages:
        joined = parts[0] if len(parts) == 1 else jnp.concatenate(parts, axis=0)
        parts = shifted(joined, "draw", stride, factor)
    return parts


def near(*arrays):
    return [pltpu.with_memory_space_constraint(array, pltpu.VMEM) for array in arrays]


def total_of(parts):
    return functools.reduce(jnp.add, parts)


def body(product_traits, mean_utility, target, taste_scale, taste_draws, outside, block_market):
    k_count, prod_count = product_traits.shape
    group = taste_draws.shape[1]
    draw_devices = lax.axis_size("draw")
    prod_devices = lax.axis_size("prod")
    draws = group * draw_devices
    market_scale = float(prod_count * prod_devices // MARKETS)
    share_scale = market_scale / float(draws)
    part_len = prod_count // draw_devices
    depth = 3 * k_count + 16
    tile_rows = MARKETS * group // LANES
    cells = prod_count * group

    level_rows = mean_utility.reshape(-1, LANES)
    target_rows = target.reshape(-1, LANES)
    scale_row = taste_scale.reshape(1, k_count)

    stages = []
    stride = 1
    while stride < draw_devices:
        factor = 2 if stride == 1 else math.gcd(4, draw_devices // stride)
        stages.append((stride, factor))
        stride *= factor

    def grant(rest):
        return 4 * (draws * MARKETS * 16 + BLOCK * rest + 2**19)

    fixed = 2 * depth * draws + 2 * LANES * part_len
    eighths = max(
        count for count in range(1, 8) if fixed + draws // 8 * count * part_len * 4 + grant(draws - draws // 8 * count) < BUDGET
    )
    kept = draws // 8 * eighths
    rest = draws - kept
    bounds = [draws // 8 * (eighths * index // PIECES) for index in range(PIECES + 1)]
    held_params = pltpu.CompilerParams(vmem_limit_bytes=max(grant(rest), FLOOR))

    step_len = min(STEP_BLOCKS * BLOCK, prod_count // 2)
    steps = prod_count // step_len
    whole = lambda shape: pl.BlockSpec(shape, lambda step, market: (0,) * len(shape))

    def first(begin, count, market, before):
        arrays = (market, product_traits, level_rows, scale_row, taste_draws, before)
        return pl.pallas_call(
            functools.partial(first_sums, market_scale, begin),
            grid_spec=pltpu.PrefetchScalarGridSpec(
                num_scalar_prefetch=1,
                grid=(count,),
                in_specs=[
                    pl.BlockSpec((k_count, step_len), lambda step, market: (0, step + begin)),
                    pl.BlockSpec((step_len // LANES, LANES), lambda step, market: (step + begin, 0)),
                    whole((1, k_count)),
                    whole((k_count, group)),
                    whole(before.shape),
                ],
                out_specs=whole((tile_rows, LANES)),
                scratch_shapes=[
                    pltpu.VMEM((group, depth), BF16),
                    pltpu.VMEM((MARKETS, group, LANES), F32),
                ],
            ),
            out_shape=jax.ShapeDtypeStruct((tile_rows, LANES), F32),
            compiler_params=params((k_count, step_len), (k_count, step_len), (MARKETS, group, LANES), (BLOCK, step_len), (2**20,)),
            cost_estimate=pl.CostEstimate(
                flops=2 * cells * 256 * count // steps,
                bytes_accessed=4 * k_count * step_len * count,
                transcendentals=cells * count // steps,
            ),
            name="first_sums",
        )(*[pltpu.with_memory_space_constraint(array, pltpu.HBM) for array in arrays])

    every_draw = lax.all_to_all(
        jnp.broadcast_to(taste_draws[None], (draw_devices, k_count, group)), "draw", 0, 0
    )
    denominators = first(0, steps, block_market, outside)
    denominators, every_draw = lax.optimization_barrier((denominators, every_draw))

    sums = collected([total_of(shifted(denominators, "prod", 1, prod_devices))[None]], stages)

    hbm_traits = pltpu.with_memory_space_constraint(product_traits, pltpu.HBM)
    traits_split = pl.pallas_call(
        split_products,
        in_specs=[ANY, VMEM],
        out_specs=VMEM,
        out_shape=pltpu.VMEM((part_len, depth), BF16),
        scratch_shapes=[pltpu.VMEM((k_count, part_len), F32), pltpu.SemaphoreType.DMA],
        compiler_params=params((k_count, part_len), (prod_count,), (depth, part_len)),
        name="split_products",
    )(hbm_traits, level_rows)
    draws_split = pl.pallas_call(
        functools.partial(split_draws, stages),
        in_specs=[VMEM, VMEM],
        out_specs=VMEM,
        out_shape=pltpu.VMEM((depth, draws), BF16),
        compiler_params=params((k_count, draws), (depth, draws)),
        name="split_draws",
    )(scale_row, every_draw)
    traits_split, draws_split = near(traits_split, draws_split)
    expo = []
    for begin, end in zip(bounds, bounds[1:]):
        piece = pl.pallas_call(
            functools.partial(fill, begin),
            in_specs=[VMEM, VMEM],
            out_specs=VMEM,
            out_shape=pltpu.VMEM((part_len, end - begin), F32),
            compiler_params=held_params,
            cost_estimate=pl.CostEstimate(
                flops=2 * part_len * (end - begin) * 256, bytes_accessed=2**20, transcendentals=part_len * (end - begin)
            ),
            name="fill",
        )(traits_split, draws_split)
        expo.extend(near(piece))
    held = (traits_split, draws_split, *expo)

    share, partial = pl.pallas_call(
        functools.partial(both_sums, market_scale, share_scale, stages, (len(sums), len(expo))),
        in_specs=[SMEM] + [VMEM] * (len(sums) + 4 + len(expo)),
        out_specs=(VMEM, VMEM),
        out_shape=(
            pltpu.VMEM((BLOCK, LANES), F32),
            pltpu.VMEM((draw_devices, tile_rows, LANES), F32),
        ),
        scratch_shapes=[
            pltpu.VMEM((MARKETS, 8, draws), F32),
            pltpu.VMEM((MARKETS, 8, draws), F32),
            pltpu.VMEM((BLOCK, LANES), F32),
            pltpu.VMEM((BLOCK, rest), F32),
        ],
        compiler_params=held_params,
        cost_estimate=pl.CostEstimate(flops=4 * cells, bytes_accessed=2**20, transcendentals=0),
        name="both_sums",
    )(block_market, *near(*sums), target_rows, outside, *held)

    parts = shifted(partial, "prod", 1, prod_devices)
    for stride, factor in stages:
        parts = shifted(total_of(parts), "draw", stride, factor)

    level, residual = pl.pallas_call(
        functools.partial(last_sums, share_scale, stages, (len(parts), len(expo))),
        in_specs=[SMEM] + [VMEM] * (len(parts) + 4 + len(expo) + 1),
        out_specs=(VMEM, VMEM),
        out_shape=(jax.ShapeDtypeStruct((part_len // LANES, LANES), F32),) * 2,
        scratch_shapes=[
            pltpu.VMEM((MARKETS, 8, draws), F32),
            pltpu.VMEM((BLOCK, LANES), F32),
            pltpu.VMEM((BLOCK, rest), F32),
        ],
        compiler_params=held_params,
        cost_estimate=pl.CostEstimate(flops=2 * cells, bytes_accessed=2**20, transcendentals=0),
        name="last_sums",
    )(block_market, *near(*parts), target_rows, level_rows, *held, *near(share))
    return level.reshape(-1), residual.reshape(-1)


def solution(mesh):
    placed = (
        P(None, "prod"),
        P("prod"),
        P("prod"),
        P(),
        P(None, "draw"),
        P(None, "draw"),
        P("prod"),
    )
    return jax.shard_map(
        body,
        mesh=mesh,
        in_specs=placed,
        out_specs=(P(("prod", "draw")), P(("prod", "draw"))),
        check_vma=False,
    )
```

```python
import functools
import math

import jax
import jax.numpy as jnp
from jax import lax
from jax.experimental import pallas as pl
from jax.experimental.pallas import tpu as pltpu
from jax.sharding import PartitionSpec as P

MARKETS = 4
BLOCK = 256
LANES = 128
HALVES = BLOCK // LANES
LOG2E = math.log2(math.e)
BUDGET = 58 * 2**20
FLOOR = 10 * 2**20
PIECES = 3
STEP_BLOCKS = 64
F32 = jnp.float32
BF16 = jnp.bfloat16
VMEM = pl.BlockSpec(memory_space=pltpu.VMEM)
SMEM = pl.BlockSpec(memory_space=pltpu.SMEM)
ANY = pl.BlockSpec(memory_space=pl.ANY)


def params(*shapes):
    return pltpu.CompilerParams(vmem_limit_bytes=sum(4 * math.prod(shape) for shape in shapes) + 2**20)


def rounded(values):
    return values.astype(BF16).astype(F32)


def top_rows(rows, columns):
    index = lax.broadcasted_iota(jnp.int32, (16, columns), 0)
    tile = jnp.zeros((16, columns), F32)
    for place, row in enumerate(rows):
        tile = jnp.where(index == place, row, tile)
    return tile


def trait_rows(traits, level):
    first = rounded(traits)
    second = traits - first
    scaled = level * LOG2E
    one = rounded(scaled)
    two = rounded(scaled - one)
    three = scaled - one - two
    return [first, second, first, top_rows((one, two, three), traits.shape[1])]


def taste_rows(taste_draws, scale_row):
    k_count, columns = taste_draws.shape
    diagonal = lax.broadcasted_iota(jnp.int32, (k_count, k_count), 0) == lax.broadcasted_iota(
        jnp.int32, (k_count, k_count), 1
    )
    scale = jnp.sum(jnp.where(diagonal, scale_row, 0.0), axis=1, keepdims=True)
    mix = scale * taste_draws * LOG2E
    first = rounded(mix)
    second = mix - first
    one = jnp.ones((1, columns), F32)
    return [first, first, second, top_rows((one, one, one), columns)]


def stacked(rows):
    return jnp.concatenate([row.astype(BF16) for row in rows], axis=0)


def level_row(level_ref, block):
    return jnp.concatenate(
        [level_ref[pl.ds(block * HALVES + half, 1), :] for half in range(HALVES)], axis=1
    )


def mm(left, right):
    return lax.dot_general(left, right, (((1,), (0,)), ((), ())), preferred_element_type=F32)


def first_sums(market_scale, begin, market_ref, traits_ref, level_ref, scale_ref, draws_ref, before_ref, sums_ref, left, total):
    step = pl.program_id(0)

    @pl.when(step == 0)
    def _():
        rows = jnp.concatenate(taste_rows(draws_ref[...], scale_ref[...]), axis=0)
        left[...] = rows.T.astype(BF16)
        total[...] = jnp.zeros_like(total)

    for local in range(traits_ref.shape[1] // BLOCK):
        block = (begin + step) * (traits_ref.shape[1] // BLOCK) + local
        right = stacked(
            trait_rows(traits_ref[:, local * BLOCK : (local + 1) * BLOCK], level_row(level_ref, local))
        )
        expo = jnp.exp2(mm(left[...], right))
        part = expo[:, :LANES]
        for half in range(1, HALVES):
            part = part + expo[:, half * LANES : (half + 1) * LANES]
        market = market_ref[block]
        total[market] += part

    @pl.when(step == pl.num_programs(0) - 1)
    def _():
        if begin == 0:
            own = jnp.where(lax.axis_index("prod") == 0, market_scale, 0.0)
            outer = own * jnp.exp(before_ref[...])
        ones = jnp.ones((8, LANES), F32)
        pieces = []
        for market in range(MARKETS):
            summed = lax.dot_general(
                ones,
                total[market],
                (((1,), (1,)), ((), ())),
                precision=lax.Precision.HIGHEST,
                preferred_element_type=F32,
            )
            row = summed[0:1, :]
            if begin == 0:
                row = row + outer[market : market + 1, :]
            for half in range(row.shape[1] // LANES):
                pieces.append(row[:, half * LANES : (half + 1) * LANES])
        tile = jnp.concatenate(pieces, axis=0)
        sums_ref[...] = tile if begin == 0 else tile + before_ref[...]


def split_products(traits_hbm, level_hbm, traits_out, traits_vmem, level_vmem, arrived):
    part_len = traits_vmem.shape[1]
    own = lax.axis_index("draw")
    rows = part_len // LANES
    copies = (
        pltpu.make_async_copy(
            traits_hbm.at[:, pl.ds(pl.multiple_of(own * part_len, part_len), part_len)], traits_vmem, arrived.at[0]
        ),
        pltpu.make_async_copy(
            level_hbm.at[pl.ds(pl.multiple_of(own * rows, rows), rows), :], level_vmem, arrived.at[1]
        ),
    )
    for copy in copies:
        copy.start()
    for copy in copies:
        copy.wait()
    blocks = part_len // BLOCK

    def step(block, carry):
        start = pl.multiple_of(block * BLOCK, BLOCK)
        rows = trait_rows(traits_vmem[:, pl.ds(start, BLOCK)], level_row(level_vmem, block))
        traits_out[pl.ds(start, BLOCK), :] = jnp.concatenate(rows, axis=0).T.astype(BF16)
        return carry

    lax.fori_loop(0, blocks, step, 0, unroll=4)


def group_at(place, stages):
    own = lax.axis_index("draw")
    group = own
    for stride, factor in stages:
        digit = lax.rem(own // stride, factor)
        shift = place % factor
        place //= factor
        group = group + (lax.rem(digit - shift + factor, factor) - digit) * stride
    return group


def split_draws(stages, scale_ref, draws_ref, right_out):
    group = draws_ref.shape[2]
    for place in range(draws_ref.shape[0]):
        rows = taste_rows(draws_ref[group_at(place, stages)], scale_ref[...])
        right_out[:, place * group : (place + 1) * group] = stacked(rows)


def fill(offset, traits_ref, right_ref, expo_ref):
    blocks, kept = expo_ref.shape[0] // BLOCK, expo_ref.shape[1]

    def step(block, carry):
        start = pl.multiple_of(block * BLOCK, BLOCK)
        left = traits_ref[pl.ds(start, BLOCK), :]

        def columns(begin):
            expo_ref[pl.ds(start, BLOCK), pl.ds(begin, 256)] = jnp.exp2(mm(left, right_ref[:, pl.ds(offset + begin, 256)]))

        if kept <= 2048:
            for begin in range(0, kept, 256):
                columns(begin)
        else:

            def inner(index, carry):
                columns(pl.multiple_of(index * 256, 256))
                return carry

            lax.fori_loop(0, kept // 256, inner, 0)
        return carry

    lax.fori_loop(0, blocks, step, 0, unroll=4)


def inverse_rows(inverse, pieces):
    for group, tile in enumerate(pieces):
        flipped = 1.0 / tile
        halves = tile.shape[0] // MARKETS
        for market in range(MARKETS):
            for half in range(halves):
                row = market * halves + half
                start = (group * halves + half) * LANES
                inverse[market, :, start : start + LANES] = jnp.broadcast_to(flipped[row : row + 1, :], (8, LANES))


def over_columns(width, body, carry):
    tiles = width // LANES
    if tiles <= 16:
        for tile in range(tiles):
            carry = body(tile * LANES, carry)
        return carry
    return lax.fori_loop(0, tiles, lambda tile, kept: body(pl.multiple_of(tile * LANES, LANES), kept), carry)


def share_sum(expo_refs, rest_expo, inverse, market, start):
    total = jnp.zeros((BLOCK // 8, 8, LANES), F32)
    offset = 0
    for ref in expo_refs + (rest_expo,):
        first = 0 if ref is rest_expo else start

        def columns(begin, total, ref=ref, first=first, offset=offset):
            terms = ref[pl.ds(first, BLOCK), pl.ds(begin, LANES)].reshape(BLOCK // 8, 8, LANES)
            return total + terms * inverse[market, :, pl.ds(offset + begin, LANES)]

        total = over_columns(ref.shape[1], columns, total)
        offset += ref.shape[1]
    return jnp.sum(total.reshape(BLOCK, LANES), axis=1, keepdims=True)


def rest_columns_of(rest_expo, traits_ref, rest_ref, start):
    left = traits_ref[pl.ds(start, BLOCK), :]
    for begin in range(0, rest_expo.shape[1], 256):
        rest_expo[:, begin : begin + 256] = jnp.exp2(mm(left, rest_ref[:, pl.ds(rest_ref.shape[1] - rest_expo.shape[1] + begin, 256)]))


def own_rows(ref, blocks):
    base = lax.axis_index("draw") * (blocks * HALVES)
    return jnp.concatenate(
        [ref[pl.ds(base + half, blocks, stride=HALVES), :] for half in range(HALVES)], axis=1
    )


def both_sums(market_scale, share_scale, stages, counts, market_ref, *refs):
    sums_refs, refs = refs[: counts[0]], refs[counts[0] :]
    (target_ref, outside_ref, traits_ref, right_ref), refs = refs[:4], refs[4:]
    expo_refs, refs = refs[: counts[1]], refs[counts[1] :]
    share_ref, next_ref, inverse, total, growth, rest_expo = refs
    blocks = expo_refs[0].shape[0] // BLOCK
    groups = next_ref.shape[0]
    own = lax.axis_index("draw")
    inverse_rows(inverse, [ref[place] for ref in sums_refs for place in range(ref.shape[0])])
    total[...] = jnp.zeros_like(total)
    wanted = jnp.exp(own_rows(target_ref, blocks)) / share_scale
    if blocks < LANES:
        wanted = jnp.concatenate([wanted, jnp.ones((LANES - blocks, BLOCK), F32)], axis=0)
    growth[...] = wanted.T
    share_ref[...] = jnp.ones_like(share_ref)
    lane = lax.broadcasted_iota(jnp.int32, (BLOCK, LANES), 1)

    def step(block, carry):
        start = pl.multiple_of(block * BLOCK, BLOCK)
        market = market_ref[own * blocks + block]
        rest_columns_of(rest_expo, traits_ref, right_ref, start)
        share = share_sum(expo_refs, rest_expo, inverse, market, start)
        here = lane == block
        factor = jnp.sum(jnp.where(here, growth[...], 0.0), axis=1, keepdims=True)
        share_ref[...] = jnp.where(here, share, share_ref[...])
        factor = jnp.broadcast_to(factor / share, (BLOCK, LANES))
        offset = 0
        for ref in expo_refs + (rest_expo,):
            first = 0 if ref is rest_expo else start

            def columns(begin, carry, ref=ref, first=first, offset=offset):
                terms = ref[pl.ds(first, BLOCK), pl.ds(begin, LANES)] * factor
                total[market, :, pl.ds(offset + begin, LANES)] += terms.reshape(BLOCK // 8, 8, LANES).sum(axis=0)
                return carry

            over_columns(ref.shape[1], columns, 0)
            offset += ref.shape[1]
        return carry

    lax.fori_loop(0, blocks, step, 0, unroll=4)
    halves = next_ref.shape[1] // MARKETS
    mine = jnp.where(lax.axis_index("prod") == 0, market_scale, 0.0)
    outer = mine * jnp.exp(outside_ref[...])
    for place in range(groups):
        rows = []
        for market in range(MARKETS):
            for half in range(halves):
                begin = (place * halves + half) * LANES
                row = jnp.sum(total[market, :, begin : begin + LANES], axis=0, keepdims=True)
                if place == 0:
                    row = row + outer[market : market + 1, half * LANES : (half + 1) * LANES]
                rows.append(row)
        next_ref[group_at(place, stages)] = jnp.concatenate(rows, axis=0)


def last_sums(share_scale, stages, counts, market_ref, *refs):
    sums_refs, refs = refs[: counts[0]], refs[counts[0] :]
    (target_ref, level_ref, traits_ref, right_ref), refs = refs[:4], refs[4:]
    expo_refs, refs = refs[: counts[1]], refs[counts[1] :]
    share_ref, out_level, out_residual, inverse, second, rest_expo = refs
    blocks = expo_refs[0].shape[0] // BLOCK
    own = lax.axis_index("draw")
    pieces = []
    for place in range(sums_refs[0].shape[0]):
        group = group_at(place, stages)
        tile = sums_refs[0][group]
        for ref in sums_refs[1:]:
            tile = tile + ref[group]
        pieces.append(tile)
    inverse_rows(inverse, pieces)
    second[...] = jnp.ones_like(second)
    lane = lax.broadcasted_iota(jnp.int32, (BLOCK, LANES), 1)

    def step(block, carry):
        start = pl.multiple_of(block * BLOCK, BLOCK)
        market = market_ref[own * blocks + block]
        rest_columns_of(rest_expo, traits_ref, right_ref, start)
        share = share_sum(expo_refs, rest_expo, inverse, market, start)
        second[...] = jnp.where(lane == block, share, second[...])
        return carry

    lax.fori_loop(0, blocks, step, 0, unroll=8)
    before = share_ref[...].T[:blocks]
    after = second[...].T[:blocks]
    residual = jnp.log(before) - jnp.log(after)
    level = own_rows(level_ref, blocks) + own_rows(target_ref, blocks) - jnp.log(after * share_scale)
    for half in range(HALVES):
        columns = slice(half * LANES, (half + 1) * LANES)
        out_residual[pl.ds(half, blocks, stride=HALVES), :] = residual[:, columns]
        out_level[pl.ds(half, blocks, stride=HALVES), :] = level[:, columns]


def digit_pairs(size, stride, factor, shift):
    pairs = []
    for index in range(size):
        digit = index // stride % factor
        pairs.append((index, index + ((digit + shift) % factor - digit) * stride))
    return pairs


def shifted(values, axis, stride, factor):
    size = lax.axis_size(axis)
    return [values] + [
        lax.ppermute(values, axis, digit_pairs(size, stride, factor, shift)) for shift in range(1, factor)
    ]


def collected(parts, stages):
    for stride, factor in stages:
        joined = parts[0] if len(parts) == 1 else jnp.concatenate(parts, axis=0)
        parts = shifted(joined, "draw", stride, factor)
    return parts


def near(*arrays):
    return [pltpu.with_memory_space_constraint(array, pltpu.VMEM) for array in arrays]


def total_of(parts):
    return functools.reduce(jnp.add, parts)


def body(product_traits, mean_utility, target, taste_scale, taste_draws, outside, block_market):
    k_count, prod_count = product_traits.shape
    group = taste_draws.shape[1]
    draw_devices = lax.axis_size("draw")
    prod_devices = lax.axis_size("prod")
    draws = group * draw_devices
    market_scale = float(prod_count * prod_devices // MARKETS)
    share_scale = market_scale / float(draws)
    part_len = prod_count // draw_devices
    depth = 3 * k_count + 16
    tile_rows = MARKETS * group // LANES
    cells = prod_count * group

    level_rows = mean_utility.reshape(-1, LANES)
    target_rows = target.reshape(-1, LANES)
    scale_row = taste_scale.reshape(1, k_count)

    stages = []
    stride = 1
    while stride < draw_devices:
        factor = 2 if stride == 1 else math.gcd(4, draw_devices // stride)
        stages.append((stride, factor))
        stride *= factor

    def grant(rest):
        return 4 * (draws * MARKETS * 16 + BLOCK * rest + 2**19)

    fixed = 2 * depth * draws + 2 * LANES * part_len
    eighths = max(
        count for count in range(1, 8) if fixed + draws // 8 * count * part_len * 4 + grant(draws - draws // 8 * count) < BUDGET
    )
    kept = draws // 8 * eighths
    rest = draws - kept
    bounds = [draws // 8 * (eighths * index // PIECES) for index in range(PIECES + 1)]
    held_params = pltpu.CompilerParams(vmem_limit_bytes=max(grant(rest), FLOOR))

    step_len = min(STEP_BLOCKS * BLOCK, prod_count // 2)
    steps = prod_count // step_len
    whole = lambda shape: pl.BlockSpec(shape, lambda step, market: (0,) * len(shape))

    def first(begin, count, market, before):
        arrays = (market, product_traits, level_rows, scale_row, taste_draws, before)
        return pl.pallas_call(
            functools.partial(first_sums, market_scale, begin),
            grid_spec=pltpu.PrefetchScalarGridSpec(
                num_scalar_prefetch=1,
                grid=(count,),
                in_specs=[
                    pl.BlockSpec((k_count, step_len), lambda step, market: (0, step + begin)),
                    pl.BlockSpec((step_len // LANES, LANES), lambda step, market: (step + begin, 0)),
                    whole((1, k_count)),
                    whole((k_count, group)),
                    whole(before.shape),
                ],
                out_specs=whole((tile_rows, LANES)),
                scratch_shapes=[
                    pltpu.VMEM((group, depth), BF16),
                    pltpu.VMEM((MARKETS, group, LANES), F32),
                ],
            ),
            out_shape=jax.ShapeDtypeStruct((tile_rows, LANES), F32),
            compiler_params=params((k_count, step_len), (k_count, step_len), (MARKETS, group, LANES), (BLOCK, step_len), (2**20,)),
            cost_estimate=pl.CostEstimate(
                flops=2 * cells * 256 * count // steps,
                bytes_accessed=4 * k_count * step_len * count,
                transcendentals=cells * count // steps,
            ),
            name="first_sums",
        )(*[pltpu.with_memory_space_constraint(array, pltpu.HBM) for array in arrays])

    every_draw = lax.all_to_all(
        jnp.broadcast_to(taste_draws[None], (draw_devices, k_count, group)), "draw", 0, 0
    )
    denominators = first(0, steps, block_market, outside)
    denominators, every_draw = lax.optimization_barrier((denominators, every_draw))

    sums = collected([total_of(shifted(denominators, "prod", 1, prod_devices))[None]], stages)

    hbm_traits = pltpu.with_memory_space_constraint(product_traits, pltpu.HBM)
    traits_split = pl.pallas_call(
        split_products,
        in_specs=[ANY, ANY],
        out_specs=VMEM,
        out_shape=pltpu.VMEM((part_len, depth), BF16),
        scratch_shapes=[
            pltpu.VMEM((k_count, part_len), F32),
            pltpu.VMEM((part_len // LANES, LANES), F32),
            pltpu.SemaphoreType.DMA((2,)),
        ],
        compiler_params=params((k_count, part_len), (prod_count,), (depth, part_len)),
        name="split_products",
    )(hbm_traits, pltpu.with_memory_space_constraint(level_rows, pltpu.HBM))
    draws_split = pl.pallas_call(
        functools.partial(split_draws, stages),
        in_specs=[VMEM, VMEM],
        out_specs=VMEM,
        out_shape=pltpu.VMEM((depth, draws), BF16),
        compiler_params=params((k_count, draws), (depth, draws)),
        name="split_draws",
    )(scale_row, every_draw)
    traits_split, draws_split = near(traits_split, draws_split)
    expo = []
    for begin, end in zip(bounds, bounds[1:]):
        piece = pl.pallas_call(
            functools.partial(fill, begin),
            in_specs=[VMEM, VMEM],
            out_specs=VMEM,
            out_shape=pltpu.VMEM((part_len, end - begin), F32),
            compiler_params=held_params,
            cost_estimate=pl.CostEstimate(
                flops=2 * part_len * (end - begin) * 256, bytes_accessed=2**20, transcendentals=part_len * (end - begin)
            ),
            name="fill",
        )(traits_split, draws_split)
        expo.extend(near(piece))
    held = (traits_split, draws_split, *expo)

    share, partial = pl.pallas_call(
        functools.partial(both_sums, market_scale, share_scale, stages, (len(sums), len(expo))),
        in_specs=[SMEM] + [VMEM] * (len(sums) + 4 + len(expo)),
        out_specs=(VMEM, VMEM),
        out_shape=(
            pltpu.VMEM((BLOCK, LANES), F32),
            pltpu.VMEM((draw_devices, tile_rows, LANES), F32),
        ),
        scratch_shapes=[
            pltpu.VMEM((MARKETS, 8, draws), F32),
            pltpu.VMEM((MARKETS, 8, draws), F32),
            pltpu.VMEM((BLOCK, LANES), F32),
            pltpu.VMEM((BLOCK, rest), F32),
        ],
        compiler_params=held_params,
        cost_estimate=pl.CostEstimate(flops=4 * cells, bytes_accessed=2**20, transcendentals=0),
        name="both_sums",
    )(block_market, *near(*sums), target_rows, outside, *held)

    parts = shifted(partial, "prod", 1, prod_devices)
    for stride, factor in stages:
        parts = shifted(total_of(parts), "draw", stride, factor)

    level, residual = pl.pallas_call(
        functools.partial(last_sums, share_scale, stages, (len(parts), len(expo))),
        in_specs=[SMEM] + [VMEM] * (len(parts) + 4 + len(expo) + 1),
        out_specs=(VMEM, VMEM),
        out_shape=(jax.ShapeDtypeStruct((part_len // LANES, LANES), F32),) * 2,
        scratch_shapes=[
            pltpu.VMEM((MARKETS, 8, draws), F32),
            pltpu.VMEM((BLOCK, LANES), F32),
            pltpu.VMEM((BLOCK, rest), F32),
        ],
        compiler_params=held_params,
        cost_estimate=pl.CostEstimate(flops=2 * cells, bytes_accessed=2**20, transcendentals=0),
        name="last_sums",
    )(block_market, *near(*parts), target_rows, level_rows, *held, *near(share))
    return level.reshape(-1), residual.reshape(-1)


def solution(mesh):
    placed = (
        P(None, "prod"),
        P("prod"),
        P("prod"),
        P(),
        P(None, "draw"),
        P(None, "draw"),
        P("prod"),
    )
    return jax.shard_map(
        body,
        mesh=mesh,
        in_specs=placed,
        out_specs=(P(("prod", "draw")), P(("prod", "draw"))),
        check_vma=False,
    )
```

```python
import functools
import math

import jax
import jax.numpy as jnp
from jax import lax
from jax.experimental import pallas as pl
from jax.experimental.pallas import tpu as pltpu
from jax.sharding import PartitionSpec as P

MARKETS = 4
BLOCK = 256
LANES = 128
HALVES = BLOCK // LANES
LOG2E = math.log2(math.e)
BUDGET = 58 * 2**20
FLOOR = 10 * 2**20
PIECES = 3
STEP_BLOCKS = 64
F32 = jnp.float32
BF16 = jnp.bfloat16
VMEM = pl.BlockSpec(memory_space=pltpu.VMEM)
SMEM = pl.BlockSpec(memory_space=pltpu.SMEM)
ANY = pl.BlockSpec(memory_space=pl.ANY)


def params(*shapes):
    return pltpu.CompilerParams(vmem_limit_bytes=sum(4 * math.prod(shape) for shape in shapes) + 2**20)


def rounded(values):
    return values.astype(BF16).astype(F32)


def top_rows(rows, columns):
    index = lax.broadcasted_iota(jnp.int32, (16, columns), 0)
    tile = jnp.zeros((16, columns), F32)
    for place, row in enumerate(rows):
        tile = jnp.where(index == place, row, tile)
    return tile


def trait_rows(traits, level):
    first = rounded(traits)
    second = traits - first
    scaled = level * LOG2E
    one = rounded(scaled)
    two = rounded(scaled - one)
    three = scaled - one - two
    return [first, second, first, top_rows((one, two, three), traits.shape[1])]


def taste_rows(taste_draws, scale_row):
    k_count, columns = taste_draws.shape
    diagonal = lax.broadcasted_iota(jnp.int32, (k_count, k_count), 0) == lax.broadcasted_iota(
        jnp.int32, (k_count, k_count), 1
    )
    scale = jnp.sum(jnp.where(diagonal, scale_row, 0.0), axis=1, keepdims=True)
    mix = scale * taste_draws * LOG2E
    first = rounded(mix)
    second = mix - first
    one = jnp.ones((1, columns), F32)
    return [first, first, second, top_rows((one, one, one), columns)]


def stacked(rows):
    return jnp.concatenate([row.astype(BF16) for row in rows], axis=0)


def level_row(level_ref, block):
    return jnp.concatenate(
        [level_ref[pl.ds(block * HALVES + half, 1), :] for half in range(HALVES)], axis=1
    )


def mm(left, right):
    return lax.dot_general(left, right, (((1,), (0,)), ((), ())), preferred_element_type=F32)


def first_sums(market_scale, begin, market_ref, traits_ref, level_ref, scale_ref, draws_ref, before_ref, sums_ref, left, total):
    step = pl.program_id(0)

    @pl.when(step == 0)
    def _():
        rows = jnp.concatenate(taste_rows(draws_ref[...], scale_ref[...]), axis=0)
        left[...] = rows.T.astype(BF16)
        total[...] = jnp.zeros_like(total)

    for local in range(traits_ref.shape[1] // BLOCK):
        block = (begin + step) * (traits_ref.shape[1] // BLOCK) + local
        right = stacked(
            trait_rows(traits_ref[:, local * BLOCK : (local + 1) * BLOCK], level_row(level_ref, local))
        )
        expo = jnp.exp2(mm(left[...], right))
        part = expo[:, :LANES]
        for half in range(1, HALVES):
            part = part + expo[:, half * LANES : (half + 1) * LANES]
        market = market_ref[block]
        total[market] += part

    @pl.when(step == pl.num_programs(0) - 1)
    def _():
        if begin == 0:
            own = jnp.where(lax.axis_index("prod") == 0, market_scale, 0.0)
            outer = own * jnp.exp(before_ref[...])
        ones = jnp.ones((8, LANES), F32)
        pieces = []
        for market in range(MARKETS):
            summed = lax.dot_general(
                ones,
                total[market],
                (((1,), (1,)), ((), ())),
                precision=lax.Precision.HIGHEST,
                preferred_element_type=F32,
            )
            row = summed[0:1, :]
            if begin == 0:
                row = row + outer[market : market + 1, :]
            for half in range(row.shape[1] // LANES):
                pieces.append(row[:, half * LANES : (half + 1) * LANES])
        tile = jnp.concatenate(pieces, axis=0)
        sums_ref[...] = tile if begin == 0 else tile + before_ref[...]


def split_products(traits_hbm, level_hbm, traits_out, traits_vmem, level_vmem, arrived):
    part_len = traits_vmem.shape[1]
    own = lax.axis_index("draw")
    rows = part_len // LANES
    copies = (
        pltpu.make_async_copy(
            traits_hbm.at[:, pl.ds(pl.multiple_of(own * part_len, part_len), part_len)], traits_vmem, arrived.at[0]
        ),
        pltpu.make_async_copy(
            level_hbm.at[pl.ds(pl.multiple_of(own * rows, rows), rows), :], level_vmem, arrived.at[1]
        ),
    )
    for copy in copies:
        copy.start()
    for copy in copies:
        copy.wait()
    blocks = part_len // BLOCK

    def step(block, carry):
        start = pl.multiple_of(block * BLOCK, BLOCK)
        rows = trait_rows(traits_vmem[:, pl.ds(start, BLOCK)], level_row(level_vmem, block))
        traits_out[pl.ds(start, BLOCK), :] = jnp.concatenate(rows, axis=0).T.astype(BF16)
        return carry

    lax.fori_loop(0, blocks, step, 0, unroll=4)


def group_at(place, stages):
    own = lax.axis_index("draw")
    group = own
    for stride, factor in stages:
        digit = lax.rem(own // stride, factor)
        shift = place % factor
        place //= factor
        group = group + (lax.rem(digit - shift + factor, factor) - digit) * stride
    return group


def split_draws(stages, scale_ref, draws_ref, right_out):
    group = draws_ref.shape[2]
    for place in range(draws_ref.shape[0]):
        rows = taste_rows(draws_ref[group_at(place, stages)], scale_ref[...])
        right_out[:, place * group : (place + 1) * group] = stacked(rows)


def fill(offset, traits_ref, right_ref, expo_ref):
    blocks, kept = expo_ref.shape[0] // BLOCK, expo_ref.shape[1]

    def step(block, carry):
        start = pl.multiple_of(block * BLOCK, BLOCK)
        left = traits_ref[pl.ds(start, BLOCK), :]

        def columns(begin):
            expo_ref[pl.ds(start, BLOCK), pl.ds(begin, 256)] = jnp.exp2(mm(left, right_ref[:, pl.ds(offset + begin, 256)]))

        if kept <= 2048:
            for begin in range(0, kept, 256):
                columns(begin)
        else:

            def inner(index, carry):
                columns(pl.multiple_of(index * 256, 256))
                return carry

            lax.fori_loop(0, kept // 256, inner, 0)
        return carry

    lax.fori_loop(0, blocks, step, 0, unroll=16)


def inverse_rows(inverse, pieces):
    for group, tile in enumerate(pieces):
        flipped = 1.0 / tile
        halves = tile.shape[0] // MARKETS
        for market in range(MARKETS):
            for half in range(halves):
                row = market * halves + half
                start = (group * halves + half) * LANES
                inverse[market, :, start : start + LANES] = jnp.broadcast_to(flipped[row : row + 1, :], (8, LANES))


def over_columns(width, body, carry):
    tiles = width // LANES
    if tiles <= 16:
        for tile in range(tiles):
            carry = body(tile * LANES, carry)
        return carry
    return lax.fori_loop(0, tiles, lambda tile, kept: body(pl.multiple_of(tile * LANES, LANES), kept), carry)


def share_sum(expo_refs, rest_expo, inverse, market, start):
    total = jnp.zeros((BLOCK // 8, 8, LANES), F32)
    offset = 0
    for ref in expo_refs + (rest_expo,):
        first = 0 if ref is rest_expo else start

        def columns(begin, total, ref=ref, first=first, offset=offset):
            terms = ref[pl.ds(first, BLOCK), pl.ds(begin, LANES)].reshape(BLOCK // 8, 8, LANES)
            return total + terms * inverse[market, :, pl.ds(offset + begin, LANES)]

        total = over_columns(ref.shape[1], columns, total)
        offset += ref.shape[1]
    return jnp.sum(total.reshape(BLOCK, LANES), axis=1, keepdims=True)


def rest_columns_of(rest_expo, traits_ref, rest_ref, start):
    left = traits_ref[pl.ds(start, BLOCK), :]
    for begin in range(0, rest_expo.shape[1], 256):
        rest_expo[:, begin : begin + 256] = jnp.exp2(mm(left, rest_ref[:, pl.ds(rest_ref.shape[1] - rest_expo.shape[1] + begin, 256)]))


def own_rows(ref, blocks):
    base = lax.axis_index("draw") * (blocks * HALVES)
    return jnp.concatenate(
        [ref[pl.ds(base + half, blocks, stride=HALVES), :] for half in range(HALVES)], axis=1
    )


def both_sums(market_scale, share_scale, stages, counts, market_ref, *refs):
    sums_refs, refs = refs[: counts[0]], refs[counts[0] :]
    (target_ref, outside_ref, traits_ref, right_ref), refs = refs[:4], refs[4:]
    expo_refs, refs = refs[: counts[1]], refs[counts[1] :]
    share_ref, next_ref, inverse, total, growth, rest_expo = refs
    blocks = expo_refs[0].shape[0] // BLOCK
    groups = next_ref.shape[0]
    own = lax.axis_index("draw")
    inverse_rows(inverse, [ref[place] for ref in sums_refs for place in range(ref.shape[0])])
    total[...] = jnp.zeros_like(total)
    wanted = jnp.exp(own_rows(target_ref, blocks)) / share_scale
    if blocks < LANES:
        wanted = jnp.concatenate([wanted, jnp.ones((LANES - blocks, BLOCK), F32)], axis=0)
    growth[...] = wanted.T
    share_ref[...] = jnp.ones_like(share_ref)
    lane = lax.broadcasted_iota(jnp.int32, (BLOCK, LANES), 1)

    def step(block, carry):
        start = pl.multiple_of(block * BLOCK, BLOCK)
        market = market_ref[own * blocks + block]
        rest_columns_of(rest_expo, traits_ref, right_ref, start)
        share = share_sum(expo_refs, rest_expo, inverse, market, start)
        here = lane == block
        factor = jnp.sum(jnp.where(here, growth[...], 0.0), axis=1, keepdims=True)
        share_ref[...] = jnp.where(here, share, share_ref[...])
        factor = jnp.broadcast_to(factor / share, (BLOCK, LANES))
        offset = 0
        for ref in expo_refs + (rest_expo,):
            first = 0 if ref is rest_expo else start

            def columns(begin, carry, ref=ref, first=first, offset=offset):
                terms = ref[pl.ds(first, BLOCK), pl.ds(begin, LANES)] * factor
                total[market, :, pl.ds(offset + begin, LANES)] += terms.reshape(BLOCK // 8, 8, LANES).sum(axis=0)
                return carry

            over_columns(ref.shape[1], columns, 0)
            offset += ref.shape[1]
        return carry

    lax.fori_loop(0, blocks, step, 0, unroll=4)
    halves = next_ref.shape[1] // MARKETS
    mine = jnp.where(lax.axis_index("prod") == 0, market_scale, 0.0)
    outer = mine * jnp.exp(outside_ref[...])
    for place in range(groups):
        rows = []
        for market in range(MARKETS):
            for half in range(halves):
                begin = (place * halves + half) * LANES
                row = jnp.sum(total[market, :, begin : begin + LANES], axis=0, keepdims=True)
                if place == 0:
                    row = row + outer[market : market + 1, half * LANES : (half + 1) * LANES]
                rows.append(row)
        next_ref[group_at(place, stages)] = jnp.concatenate(rows, axis=0)


def last_sums(share_scale, stages, counts, market_ref, *refs):
    sums_refs, refs = refs[: counts[0]], refs[counts[0] :]
    (target_ref, level_ref, traits_ref, right_ref), refs = refs[:4], refs[4:]
    expo_refs, refs = refs[: counts[1]], refs[counts[1] :]
    share_ref, out_level, out_residual, inverse, second, rest_expo = refs
    blocks = expo_refs[0].shape[0] // BLOCK
    own = lax.axis_index("draw")
    pieces = []
    for place in range(sums_refs[0].shape[0]):
        group = group_at(place, stages)
        tile = sums_refs[0][group]
        for ref in sums_refs[1:]:
            tile = tile + ref[group]
        pieces.append(tile)
    inverse_rows(inverse, pieces)
    second[...] = jnp.ones_like(second)
    lane = lax.broadcasted_iota(jnp.int32, (BLOCK, LANES), 1)

    def step(block, carry):
        start = pl.multiple_of(block * BLOCK, BLOCK)
        market = market_ref[own * blocks + block]
        rest_columns_of(rest_expo, traits_ref, right_ref, start)
        share = share_sum(expo_refs, rest_expo, inverse, market, start)
        second[...] = jnp.where(lane == block, share, second[...])
        return carry

    lax.fori_loop(0, blocks, step, 0, unroll=8)
    before = share_ref[...].T[:blocks]
    after = second[...].T[:blocks]
    residual = jnp.log(before) - jnp.log(after)
    level = own_rows(level_ref, blocks) + own_rows(target_ref, blocks) - jnp.log(after * share_scale)
    for half in range(HALVES):
        columns = slice(half * LANES, (half + 1) * LANES)
        out_residual[pl.ds(half, blocks, stride=HALVES), :] = residual[:, columns]
        out_level[pl.ds(half, blocks, stride=HALVES), :] = level[:, columns]


def digit_pairs(size, stride, factor, shift):
    pairs = []
    for index in range(size):
        digit = index // stride % factor
        pairs.append((index, index + ((digit + shift) % factor - digit) * stride))
    return pairs


def shifted(values, axis, stride, factor):
    size = lax.axis_size(axis)
    return [values] + [
        lax.ppermute(values, axis, digit_pairs(size, stride, factor, shift)) for shift in range(1, factor)
    ]


def collected(parts, stages):
    for stride, factor in stages:
        joined = parts[0] if len(parts) == 1 else jnp.concatenate(parts, axis=0)
        parts = shifted(joined, "draw", stride, factor)
    return parts


def near(*arrays):
    return [pltpu.with_memory_space_constraint(array, pltpu.VMEM) for array in arrays]


def total_of(parts):
    return functools.reduce(jnp.add, parts)


def body(product_traits, mean_utility, target, taste_scale, taste_draws, outside, block_market):
    k_count, prod_count = product_traits.shape
    group = taste_draws.shape[1]
    draw_devices = lax.axis_size("draw")
    prod_devices = lax.axis_size("prod")
    draws = group * draw_devices
    market_scale = float(prod_count * prod_devices // MARKETS)
    share_scale = market_scale / float(draws)
    part_len = prod_count // draw_devices
    depth = 3 * k_count + 16
    tile_rows = MARKETS * group // LANES
    cells = prod_count * group

    level_rows = mean_utility.reshape(-1, LANES)
    target_rows = target.reshape(-1, LANES)
    scale_row = taste_scale.reshape(1, k_count)

    stages = []
    stride = 1
    while stride < draw_devices:
        factor = 2 if stride == 1 else math.gcd(4, draw_devices // stride)
        stages.append((stride, factor))
        stride *= factor

    def grant(rest):
        return 4 * (draws * MARKETS * 16 + BLOCK * rest + 2**19)

    fixed = 2 * depth * draws + 2 * LANES * part_len
    eighths = max(
        count for count in range(1, 8) if fixed + draws // 8 * count * part_len * 4 + grant(draws - draws // 8 * count) < BUDGET
    )
    kept = draws // 8 * eighths
    rest = draws - kept
    bounds = [draws // 8 * (eighths * index // PIECES) for index in range(PIECES + 1)]
    held_params = pltpu.CompilerParams(vmem_limit_bytes=max(grant(rest), FLOOR))

    step_len = min(STEP_BLOCKS * BLOCK, prod_count // 2)
    steps = prod_count // step_len
    whole = lambda shape: pl.BlockSpec(shape, lambda step, market: (0,) * len(shape))

    def first(begin, count, market, before):
        arrays = (market, product_traits, level_rows, scale_row, taste_draws, before)
        return pl.pallas_call(
            functools.partial(first_sums, market_scale, begin),
            grid_spec=pltpu.PrefetchScalarGridSpec(
                num_scalar_prefetch=1,
                grid=(count,),
                in_specs=[
                    pl.BlockSpec((k_count, step_len), lambda step, market: (0, step + begin)),
                    pl.BlockSpec((step_len // LANES, LANES), lambda step, market: (step + begin, 0)),
                    whole((1, k_count)),
                    whole((k_count, group)),
                    whole(before.shape),
                ],
                out_specs=whole((tile_rows, LANES)),
                scratch_shapes=[
                    pltpu.VMEM((group, depth), BF16),
                    pltpu.VMEM((MARKETS, group, LANES), F32),
                ],
            ),
            out_shape=jax.ShapeDtypeStruct((tile_rows, LANES), F32),
            compiler_params=params((k_count, step_len), (k_count, step_len), (MARKETS, group, LANES), (BLOCK, step_len), (2**20,)),
            cost_estimate=pl.CostEstimate(
                flops=2 * cells * 256 * count // steps,
                bytes_accessed=4 * k_count * step_len * count,
                transcendentals=cells * count // steps,
            ),
            name="first_sums",
        )(*[pltpu.with_memory_space_constraint(array, pltpu.HBM) for array in arrays])

    every_draw = lax.all_to_all(
        jnp.broadcast_to(taste_draws[None], (draw_devices, k_count, group)), "draw", 0, 0
    )
    denominators = first(0, steps, block_market, outside)
    denominators, every_draw = lax.optimization_barrier((denominators, every_draw))

    sums = collected([total_of(shifted(denominators, "prod", 1, prod_devices))[None]], stages)

    hbm_traits = pltpu.with_memory_space_constraint(product_traits, pltpu.HBM)
    traits_split = pl.pallas_call(
        split_products,
        in_specs=[ANY, ANY],
        out_specs=VMEM,
        out_shape=pltpu.VMEM((part_len, depth), BF16),
        scratch_shapes=[
            pltpu.VMEM((k_count, part_len), F32),
            pltpu.VMEM((part_len // LANES, LANES), F32),
            pltpu.SemaphoreType.DMA((2,)),
        ],
        compiler_params=params((k_count, part_len), (prod_count,), (depth, part_len)),
        name="split_products",
    )(hbm_traits, pltpu.with_memory_space_constraint(level_rows, pltpu.HBM))
    draws_split = pl.pallas_call(
        functools.partial(split_draws, stages),
        in_specs=[VMEM, VMEM],
        out_specs=VMEM,
        out_shape=pltpu.VMEM((depth, draws), BF16),
        compiler_params=params((k_count, draws), (depth, draws)),
        name="split_draws",
    )(scale_row, every_draw)
    traits_split, draws_split = near(traits_split, draws_split)
    expo = []
    for begin, end in zip(bounds, bounds[1:]):
        piece = pl.pallas_call(
            functools.partial(fill, begin),
            in_specs=[VMEM, VMEM],
            out_specs=VMEM,
            out_shape=pltpu.VMEM((part_len, end - begin), F32),
            compiler_params=held_params,
            cost_estimate=pl.CostEstimate(
                flops=2 * part_len * (end - begin) * 256, bytes_accessed=2**20, transcendentals=part_len * (end - begin)
            ),
            name="fill",
        )(traits_split, draws_split)
        expo.extend(near(piece))
    held = (traits_split, draws_split, *expo)

    share, partial = pl.pallas_call(
        functools.partial(both_sums, market_scale, share_scale, stages, (len(sums), len(expo))),
        in_specs=[SMEM] + [VMEM] * (len(sums) + 4 + len(expo)),
        out_specs=(VMEM, VMEM),
        out_shape=(
            pltpu.VMEM((BLOCK, LANES), F32),
            pltpu.VMEM((draw_devices, tile_rows, LANES), F32),
        ),
        scratch_shapes=[
            pltpu.VMEM((MARKETS, 8, draws), F32),
            pltpu.VMEM((MARKETS, 8, draws), F32),
            pltpu.VMEM((BLOCK, LANES), F32),
            pltpu.VMEM((BLOCK, rest), F32),
        ],
        compiler_params=held_params,
        cost_estimate=pl.CostEstimate(flops=4 * cells, bytes_accessed=2**20, transcendentals=0),
        name="both_sums",
    )(block_market, *near(*sums), target_rows, outside, *held)

    parts = shifted(partial, "prod", 1, prod_devices)
    for stride, factor in stages:
        parts = shifted(total_of(parts), "draw", stride, factor)

    level, residual = pl.pallas_call(
        functools.partial(last_sums, share_scale, stages, (len(parts), len(expo))),
        in_specs=[SMEM] + [VMEM] * (len(parts) + 4 + len(expo) + 1),
        out_specs=(VMEM, VMEM),
        out_shape=(jax.ShapeDtypeStruct((part_len // LANES, LANES), F32),) * 2,
        scratch_shapes=[
            pltpu.VMEM((MARKETS, 8, draws), F32),
            pltpu.VMEM((BLOCK, LANES), F32),
            pltpu.VMEM((BLOCK, rest), F32),
        ],
        compiler_params=held_params,
        cost_estimate=pl.CostEstimate(flops=2 * cells, bytes_accessed=2**20, transcendentals=0),
        name="last_sums",
    )(block_market, *near(*parts), target_rows, level_rows, *held, *near(share))
    return level.reshape(-1), residual.reshape(-1)


def solution(mesh):
    placed = (
        P(None, "prod"),
        P("prod"),
        P("prod"),
        P(),
        P(None, "draw"),
        P(None, "draw"),
        P("prod"),
    )
    return jax.shard_map(
        body,
        mesh=mesh,
        in_specs=placed,
        out_specs=(P(("prod", "draw")), P(("prod", "draw"))),
        check_vma=False,
    )
```
